512 devices in a mesh: dp: 64 (over z, y), heads: 8 (over x, core).
Axes of the slice: x: 4, y: 8, z: 8, core: 2. Of those that a mesh axis runs over, the one named last changes fastest.
Arguments:
- queries: bfloat16 [64, 128, 8192], P('dp', 'heads'), may hold values from -6 to 6
- out_grad: bfloat16 [64, 128, 8192], P('dp', 'heads'), may hold values from -6 to 6
- q_gain: float32 [128], replicated, may hold values from 0.25 to 1.75
- k_gain: float32 [128], replicated, may hold values from 0.25 to 1.75
- image_keys: bfloat16 [64, 6464, 1024], P(None, 'dp', 'heads'), may hold values from -6 to 6
- image_values: bfloat16 [64, 6464, 1024], P(None, 'dp', 'heads'), may hold values from -48 to 48
- image_tiles: int32 [64], replicated, may hold values from 1 to 4, as said below
- text_len: int32 [64], replicated, may hold values from 1 to 128, as said below
Outputs:
- attention: bfloat16 [64, 128, 8192], P('dp', 'heads')
- query_grad: bfloat16 [64, 128, 8192], P('dp', 'heads')
The draws below stay inside these ranges and needn't reach their ends.
Inputs may be any that keep to these rules, and one draw needn't show every extreme that they name: `image_tiles`: the tile counts of samples 4i to 4i+3 sum to 8, and some sample has 4 tiles. `text_len`: some sample has 128 live rows.
All inputs are finite; a program needn't handle non-finite values.
Results may differ from the reference program's by a relative error of at most 0.019.
Values may be sent and summed in bfloat16 or wider, within the bound.
A program may use at most 128 MiB of HBM per device.

```python
import jax
import jax.numpy as jnp
from jax import lax

HD = 128
KV_HEADS = 8
GQ = 8
TILE = 1601
TXT = 128
SAMPLES = 64
HQ = 64
KTOK = 6464


def draw_image_tiles(key, part):
    key = jax.random.fold_in(key, 11)
    first_key, second_key = jax.random.split(key)
    patterns = jnp.array([[4, 2, 1, 1], [3, 2, 2, 1]], jnp.int32)
    groups = SAMPLES // 4
    chosen = jax.random.randint(first_key, (groups,), 0, 2)
    chosen = chosen.at[0].set(0)
    group_rows = jnp.where((chosen == 0)[:, None], patterns[0][None, :], patterns[1][None, :])
    group_keys = jax.random.split(second_key, groups)
    shuffled = jax.vmap(lambda sub_key, row_in: jax.random.permutation(sub_key, row_in))(group_keys, group_rows)
    return shuffled.reshape(SAMPLES).astype(jnp.int32)


def draw_text_len(key, part):
    key = jax.random.fold_in(key, 12)
    first_key, second_key = jax.random.split(key)
    lengths = jax.random.randint(first_key, (SAMPLES,), 1, TXT + 1)
    longest = jax.random.randint(second_key, (), 0, SAMPLES)
    lengths = jnp.where(jnp.arange(SAMPLES) == longest, TXT, lengths)
    return lengths.astype(jnp.int32)


def steps_of(stream_key, extent, pieces, smallest, largest):
    loudness, own = 1.0, jax.random.fold_in(stream_key, 6)
    for axis_at, blocks in pieces:
        steps = jnp.exp(jax.random.uniform(jax.random.fold_in(own, axis_at), (blocks,), jnp.float32, smallest / len(pieces), largest / len(pieces)))
        loudness = loudness * jnp.repeat(steps, extent[axis_at] // blocks).reshape([-1 if axis == axis_at else 1 for axis in range(len(extent))])
    return loudness


def scatter_about(key, extent, spread, most, cuts=(), held_as=jnp.bfloat16):
    loudness = steps_of(key, extent, cuts, -0.22, 0.18) if cuts else 1.0
    result = jax.random.normal(key, extent, jnp.float32) * spread * loudness
    return jnp.minimum(jnp.maximum(result, -most), most).astype(held_as)


def setup_inputs(seed: int = 0) -> dict:
    arg_keys = jax.random.split(jax.random.key(seed), 9)
    return {
        "queries": scatter_about(arg_keys[0], (SAMPLES, TXT, HQ * HD), 1.0, 6.0, ((0, 64), (1, 8))),
        "out_grad": scatter_about(arg_keys[1], (SAMPLES, TXT, HQ * HD), 1.0, 6.0, ((0, 64), (1, 8))),
        "q_gain": jnp.clip(1.0 + 0.15 * jax.random.normal(arg_keys[2], (HD,), jnp.float32), 0.25, 1.75),
        "k_gain": jnp.clip(1.0 + 0.15 * jax.random.normal(arg_keys[3], (HD,), jnp.float32), 0.25, 1.75),
        "image_keys": scatter_about(arg_keys[4], (SAMPLES, KTOK, KV_HEADS * HD), 1.0, 6.0, ((1, 64), (2, 8))),
        "image_values": scatter_about(arg_keys[5], (SAMPLES, KTOK, KV_HEADS * HD), 8.0, 48.0, ((1, 64), (2, 8))),
        "image_tiles": draw_image_tiles(jax.random.fold_in(arg_keys[8], 71), 0),
        "text_len": draw_text_len(jax.random.fold_in(arg_keys[8], 71), 0),
    }


EPSILON = 1e-05

def normalize(inputs, gain, factor):
    mean_sq = lax.optimization_barrier(jnp.mean(inputs * inputs, axis=-1, keepdims=True))
    return inputs * lax.rsqrt(mean_sq + EPSILON) * gain * factor

def rounded(inputs):
    return lax.optimization_barrier(inputs.astype(jnp.bfloat16)).astype(jnp.float32)

def reference(queries, out_grad, q_gain, k_gain, image_keys, image_values, image_tiles, text_len):
    q_scale = HD ** (-0.5)
    positions = jnp.arange(KTOK, dtype=jnp.int32)
    row_ids = jnp.arange(TXT, dtype=jnp.int32)

    def one_sample(items):
        query_rows, grad_in, key_rows, value_in, tile_count, length = items
        raw_rows = query_rows.astype(jnp.float32).reshape(TXT, KV_HEADS, GQ, HD)
        query_norm = rounded(normalize(raw_rows, q_gain, q_scale))
        key_norm = rounded(normalize(key_rows.astype(jnp.float32).reshape(KTOK, KV_HEADS, HD), k_gain, 1.0))
        value_rows = value_in.astype(jnp.float32).reshape(KTOK, KV_HEADS, HD)
        key_live = positions < tile_count * TILE
        row_live = (row_ids < length)[:, None, None, None]
        scores = jnp.einsum('tkgd,jkd->tkgj', query_norm, key_norm)
        weights = rounded(jnp.where(key_live, jnp.exp(scores), 0.0))
        totals = lax.optimization_barrier(jnp.sum(weights, axis=-1))
        attended = jnp.einsum('tkgj,jkd->tkgd', weights, value_rows) / totals[..., None]
        attended = jnp.where(row_live, attended, 0.0)
        grad_rows = jnp.where(row_live, grad_in.astype(jnp.float32).reshape(TXT, KV_HEADS, GQ, HD), 0.0)
        prob_grad = jnp.einsum('tkgd,jkd->tkgj', grad_rows, value_rows)
        deltas = lax.optimization_barrier(jnp.sum(grad_rows * attended, axis=-1))
        score_grad = rounded(weights * (prob_grad - deltas[..., None]) / totals[..., None])
        norm_grad = jnp.einsum('tkgj,jkd->tkgd', score_grad, key_norm)
        pullback = jax.vjp(lambda inputs: normalize(inputs, q_gain, q_scale), raw_rows)[1]
        query_grad = pullback(norm_grad)[0]
        return (attended.reshape(TXT, HQ * HD).astype(jnp.bfloat16), query_grad.reshape(TXT, HQ * HD).astype(jnp.bfloat16))
    attention, query_grad = lax.map(one_sample, (queries, out_grad, image_keys, image_values, image_tiles, text_len))
    return (attention, query_grad)
```

```python
import functools

import jax
import jax.numpy as jnp
from jax import lax
from jax.experimental import pallas as pl
from jax.experimental.pallas import tpu as pltpu
from jax.sharding import PartitionSpec as P

MESH = pl.DeviceIdType.MESH
EPSILON = 1e-05
TILE = 1601
HD = 128
GQ = 8
ROWS = 104
N = 8
Z_ORDER = (1, 7, 2, 6, 3, 5, 4)
Y_ORDER = (1, 7, 3, 5)
E_ORDER = (2, 6, 4)
BLOCK_ORDER = (0, 1, 7, 2, 6, 4, 3, 5)
NT = (((1,), (1,)), ((), ()))
GROUP = 256


def kernel(slots, tiles_ref, len_ref, q_ref, g_ref, qg_ref, kg_ref, p_ref, att_ref, grad_ref,
           qb, gb, i1, i2, fin, own, vk, qn, gm, acc_a, acc_b, acc_c, acc_t, ao, go,
           qs, qr, gs, gr, s1zs, s1zr, s1ys, s1yr, s2ys, s2yr, s2zs, s2zr, oas, oar, ogs, ogr, loc):
    dp = lax.axis_index("dp")
    h = lax.axis_index("heads")
    z, y = dp // N, dp % N
    par, half = y % 2, y // 2

    def zz(d):
        return (z + d) % N

    def yy(d):
        return (y + d) % N

    def at(dz, dy):
        return (zz(dz) * N + yy(dy), h)

    def hh(d):
        return (h + d) % N

    def remote(src, dst, ssem, rsem, dev):
        copy = pltpu.make_async_remote_copy(
            src_ref=src, dst_ref=dst, send_sem=ssem, recv_sem=rsem, device_id=dev, device_id_type=MESH)
        copy.start()
        return copy

    barrier = pltpu.get_barrier_semaphore()
    for d in range(1, N):
        for dev in (at(d, 0), at(0, d), (dp, hh(d))):
            pl.semaphore_signal(barrier, inc=1, device_id=dev, device_id_type=MESH)
    pl.semaphore_wait(barrier, 3 * (N - 1))

    width = GQ * HD

    def cols(i):
        return pl.ds(pl.multiple_of(i * width, width), width)

    c1 = {}
    order = (("z", 1), ("y", 1), ("z", 7), ("z", 2), ("y", 7), ("z", 6), ("z", 3), ("y", 3), ("z", 5), ("z", 4), ("y", 5))
    sent = []
    for kind, d in order:
        if kind == "z":
            c1[kind, d] = remote(p_ref.at[zz(d), par], i1.at[d - 1], s1zs.at[d - 1], s1zr.at[d - 1], at(d, 0))
        else:
            c1[kind, d] = remote(p_ref.at[:, yy(d) % 2, yy(d) // 2], i2.at[d // 2], s1ys.at[d // 2], s1yr.at[d // 2], at(0, d))
        sent.append(c1[kind, d])
    cq = []
    for d in range(1, N):
        cq.append(remote(q_ref.at[0, :, cols(hh(d))], qb.at[h], qs.at[d - 1], qr.at[d - 1], (dp, hh(d))))
        cq.append(remote(g_ref.at[0, :, cols(hh(d))], gb.at[h], gs.at[d - 1], gr.at[d - 1], (dp, hh(d))))
    sent += cq
    locals_ = [
        pltpu.make_async_copy(q_ref.at[0, :, cols(h)], qb.at[h], loc.at[0]),
        pltpu.make_async_copy(g_ref.at[0, :, cols(h)], gb.at[h], loc.at[1]),
        pltpu.make_async_copy(p_ref.at[z, par, half], own, loc.at[2]),
    ]
    for copy in locals_:
        copy.start()

    c2 = {}

    def forward_y(dz):
        for dy in E_ORDER:
            src = p_ref.at[z, par, yy(dy) // 2] if dz == 0 else i1.at[dz - 1, yy(dy) // 2]
            i = dy // 2 - 1
            c2[dy, dz] = remote(src, fin.at[i, dz], s2ys.at[i, dz], s2yr.at[i, dz], at(0, dy))
            sent.append(c2[dy, dz])

    def forward_z(dy):
        i = dy // 2
        for dz in Z_ORDER:
            c2[dy, dz] = remote(i2.at[i, zz(dz)], fin.at[3 + i, dz], s2zs.at[i, dz - 1], s2zr.at[i, dz - 1], at(dz, 0))
            sent.append(c2[dy, dz])

    forward_y(0)

    for copy in locals_:
        copy.wait()
    for copy in cq:
        copy.wait_recv()
    length = len_ref[dp]
    limit = tiles_ref[dp] * TILE
    row_live = lax.broadcasted_iota(jnp.int32, (N * 16, HD), 0) < length
    q_gain = qg_ref[...] * (HD ** -0.5)

    def raw(ref, g):
        return ref[:, :, g * HD:(g + 1) * HD].reshape(N * 16, HD).astype(jnp.float32)

    for g in range(GQ):
        here = slice(g * N * 16, (g + 1) * N * 16)
        q = raw(qb, g)
        mean_sq = jnp.mean(q * q, axis=-1, keepdims=True)
        qn[here, :] = (q * lax.rsqrt(mean_sq + EPSILON) * q_gain).astype(jnp.bfloat16)
        gm[here, :] = jnp.where(row_live, raw(gb, g), 0.0).astype(jnp.bfloat16)
    for ref in (acc_a, acc_b, acc_c, acc_t):
        ref[...] = jnp.zeros_like(ref)

    for kind, d in order:
        c1[kind, d].wait_recv()
        if kind == "z":
            forward_y(d)
        else:
            forward_z(d)

    k_gain = kg_ref[...]
    width_b = N * ROWS
    lane = lax.broadcasted_iota(jnp.int32, (1, width_b), 1)
    lane_dz = lane // ROWS
    lane_j = lane % ROWS

    def block(dy):
        chunks = []
        for dz in range(N):
            if dy == 0:
                chunks.append(own[...] if dz == 0 else i1[dz - 1, half])
            elif dy % 2 == 0:
                c2[dy, dz].wait_recv()
                chunks.append(fin[dy // 2 - 1, dz])
            elif dz == 0:
                chunks.append(i2[dy // 2, z])
            else:
                c2[dy, dz].wait_recv()
                chunks.append(fin[3 + dy // 2, dz])
        for i in range(0, N, 2):
            both = jnp.concatenate([chunks[i].astype(jnp.float32), chunks[i + 1].astype(jnp.float32)], axis=0)
            k = both[:, :HD]
            mean_sq = jnp.mean(k * k, axis=-1, keepdims=True)
            k = k * lax.rsqrt(mean_sq + EPSILON) * k_gain
            vk[i * ROWS:(i + 2) * ROWS, :HD] = both[:, HD:].astype(jnp.bfloat16)
            vk[i * ROWS:(i + 2) * ROWS, HD:] = k.astype(jnp.bfloat16)
        source = ((z - lane_dz + N) % N) * N + (y - dy + N) % N
        live = ((lane_j < slots) & (source * slots + lane_j < limit)).astype(jnp.float32)

        def rows(r, carry):
            here = pl.ds(pl.multiple_of(r * GROUP, GROUP), GROUP)
            q, g = qn[here, :], gm[here, :]
            s = lax.dot_general(q, vk[:, HD:], NT, preferred_element_type=jnp.float32)
            w = (jnp.exp(s) * live).astype(jnp.bfloat16)
            ac = jnp.dot(w, vk[...], preferred_element_type=jnp.float32)
            wf = w.astype(jnp.float32)
            a = acc_a[here, :] + ac[:, :HD]
            t = acc_t[here, :] + jnp.sum(wf, axis=-1, keepdims=True)
            d0 = jnp.sum(g.astype(jnp.float32) * a, axis=-1, keepdims=True) / jnp.maximum(t[:, :1], 1e-30)
            pg = lax.dot_general(g, vk[:, :HD], NT, preferred_element_type=jnp.float32)
            p = (wf * (pg - d0)).astype(jnp.bfloat16)
            b = jnp.dot(p, vk[:, HD:], preferred_element_type=jnp.float32)
            acc_a[here, :] = a
            acc_t[here, :] = t
            acc_b[here, :] = acc_b[here, :] + b + d0 * ac[:, HD:]
            acc_c[here, :] = acc_c[here, :] + ac[:, HD:]
            return carry

        lax.fori_loop(0, N * 16 * GQ // GROUP, rows, 0)

    for dy in BLOCK_ORDER:
        block(dy)

    for g in range(GQ):
        here = slice(g * N * 16, (g + 1) * N * 16)
        there = slice(g * HD, (g + 1) * HD)
        t = acc_t[here, :]
        att = jnp.where(row_live, acc_a[here, :] / t, 0.0)
        ao[:, :, there] = att.astype(jnp.bfloat16).reshape(N, 16, HD)
        delta = jnp.sum(gm[here, :].astype(jnp.float32) * att, axis=-1, keepdims=True)
        norm_grad = (acc_b[here, :] - delta * acc_c[here, :]) / t
        q = raw(qb, g)
        r = lax.rsqrt(jnp.mean(q * q, axis=-1, keepdims=True) + EPSILON)
        u = norm_grad * q_gain
        dq = r * u - q * (r * r * r * jnp.mean(q * u, axis=-1, keepdims=True))
        go[:, :, there] = dq.astype(jnp.bfloat16).reshape(N, 16, HD)
    outs = []
    for d in range(1, N):
        outs.append(remote(ao.at[hh(d)], att_ref.at[0, :, cols(h)], oas.at[d - 1], oar.at[d - 1], (dp, hh(d))))
        outs.append(remote(go.at[hh(d)], grad_ref.at[0, :, cols(h)], ogs.at[d - 1], ogr.at[d - 1], (dp, hh(d))))
    mine = [
        pltpu.make_async_copy(ao.at[h], att_ref.at[0, :, cols(h)], loc.at[0]),
        pltpu.make_async_copy(go.at[h], grad_ref.at[0, :, cols(h)], loc.at[1]),
    ]
    for copy in mine:
        copy.start()
    for copy in sent:
        copy.wait_send()
    for copy in mine:
        copy.wait()
    for copy in outs:
        copy.wait()


def local(queries, out_grad, q_gain, k_gain, image_keys, image_values, image_tiles, text_len):
    samples, slots, _ = image_keys.shape
    both = jnp.concatenate([image_keys, image_values], axis=-1)
    both = jnp.pad(both, ((0, 0), (0, ROWS - slots), (0, 0)))
    packed = both.reshape(N, N // 2, 2, ROWS, 2 * HD).transpose(0, 2, 1, 3, 4)
    rows = queries.shape[1] * N
    q_rows = rows * GQ
    bf, f32 = jnp.bfloat16, jnp.float32
    dma = pltpu.SemaphoreType.DMA
    vmem = pl.BlockSpec(memory_space=pltpu.VMEM)
    smem = pl.BlockSpec(memory_space=pltpu.SMEM)
    hbm = pl.BlockSpec(memory_space=pl.ANY)
    out = jax.ShapeDtypeStruct(queries.shape, bf)

    return tuple(pl.pallas_call(
        functools.partial(kernel, slots),
        name="exchange_attention",
        out_shape=(out, out),
        in_specs=[smem, smem, hbm, hbm, vmem, vmem, hbm],
        out_specs=(hbm, hbm),
        scratch_shapes=[
            pltpu.VMEM((N, 16, GQ * HD), bf),
            pltpu.VMEM((N, 16, GQ * HD), bf),
            pltpu.VMEM((7, 4, ROWS, 2 * HD), bf),
            pltpu.VMEM((4, N, ROWS, 2 * HD), bf),
            pltpu.VMEM((7, N, ROWS, 2 * HD), bf),
            pltpu.VMEM((ROWS, 2 * HD), bf),
            pltpu.VMEM((N * ROWS, 2 * HD), bf),
            pltpu.VMEM((q_rows, HD), bf),
            pltpu.VMEM((q_rows, HD), bf),
            pltpu.VMEM((q_rows, HD), f32),
            pltpu.VMEM((q_rows, HD), f32),
            pltpu.VMEM((q_rows, HD), f32),
            pltpu.VMEM((q_rows, HD), f32),
            pltpu.VMEM((N, 16, GQ * HD), bf),
            pltpu.VMEM((N, 16, GQ * HD), bf),
            dma((7,)), dma((7,)), dma((7,)), dma((7,)),
            dma((7,)), dma((7,)), dma((4,)), dma((4,)),
            dma((3, N)), dma((3, N)), dma((4, 7)), dma((4, 7)),
            dma((7,)), dma((7,)), dma((7,)), dma((7,)),
            dma((3,)),
        ],
        compiler_params=pltpu.CompilerParams(
            collective_id=0, has_side_effects=True, vmem_limit_bytes=48 * 2 ** 20),
        cost_estimate=pl.CostEstimate(flops=8_000_000_000, bytes_accessed=8_000_000, transcendentals=7_000_000),
    )(image_tiles, text_len, queries, out_grad, q_gain.reshape(1, HD), k_gain.reshape(1, HD), packed))


def solution(mesh):
    return jax.shard_map(
        local,
        mesh=mesh,
        in_specs=(
            P("dp", "heads", None),
            P("dp", "heads", None),
            P(),
            P(),
            P(None, "dp", "heads"),
            P(None, "dp", "heads"),
            P(),
            P(),
        ),
        out_specs=(P("dp", "heads", None), P("dp", "heads", None)),
        check_vma=False,
    )
```

```python
import functools

import jax
import jax.numpy as jnp
from jax import lax
from jax.experimental import pallas as pl
from jax.experimental.pallas import tpu as pltpu
from jax.sharding import PartitionSpec as P

MESH = pl.DeviceIdType.MESH
EPSILON = 1e-05
TILE = 1601
HD = 128
GQ = 8
ROWS = 104
N = 8
Z_ORDER = (1, 7, 2, 6, 3, 5, 4)
Y_ORDER = (1, 7, 3, 5)
E_ORDER = (2, 6, 4)
BLOCK_ORDER = (0, 1, 7, 2, 6, 4, 3, 5)
NT = (((1,), (1,)), ((), ()))
GROUP = 256


def kernel(slots, tiles_ref, len_ref, q_ref, g_ref, qg_ref, kg_ref, p_ref, att_ref, grad_ref,
           qb, gb, i1, i2, fin, own, vk, qn, gm, acc_a, acc_b, acc_c, acc_t, ao, go,
           qs, qr, gs, gr, s1zs, s1zr, s1ys, s1yr, s2ys, s2yr, s2zs, s2zr, oas, oar, ogs, ogr, loc):
    dp = lax.axis_index("dp")
    h = lax.axis_index("heads")
    z, y = dp // N, dp % N
    par, half = y % 2, y // 2

    def zz(d):
        return (z + d) % N

    def yy(d):
        return (y + d) % N

    def at(dz, dy):
        return (zz(dz) * N + yy(dy), h)

    def hh(d):
        return (h + d) % N

    def remote(src, dst, ssem, rsem, dev):
        copy = pltpu.make_async_remote_copy(
            src_ref=src, dst_ref=dst, send_sem=ssem, recv_sem=rsem, device_id=dev, device_id_type=MESH)
        copy.start()
        return copy

    barrier = pltpu.get_barrier_semaphore()
    for d in range(1, N):
        for dev in (at(d, 0), at(0, d), (dp, hh(d))):
            pl.semaphore_signal(barrier, inc=1, device_id=dev, device_id_type=MESH)
    pl.semaphore_wait(barrier, 3 * (N - 1))

    width = GQ * HD

    def cols(i):
        return pl.ds(pl.multiple_of(i * width, width), width)

    c1 = {}
    order = (("z", 1), ("y", 1), ("z", 7), ("z", 2), ("y", 7), ("z", 6), ("z", 3), ("y", 3), ("z", 5), ("z", 4), ("y", 5))
    sent = []
    for kind, d in order:
        if kind == "z":
            c1[kind, d] = remote(p_ref.at[zz(d), par], i1.at[d - 1], s1zs.at[d - 1], s1zr.at[d - 1], at(d, 0))
        else:
            c1[kind, d] = remote(p_ref.at[:, yy(d) % 2, yy(d) // 2], i2.at[d // 2], s1ys.at[d // 2], s1yr.at[d // 2], at(0, d))
        sent.append(c1[kind, d])
    cq = []
    for d in range(1, N):
        cq.append(remote(q_ref.at[0, :, cols(hh(d))], qb.at[h], qs.at[d - 1], qr.at[d - 1], (dp, hh(d))))
        cq.append(remote(g_ref.at[0, :, cols(hh(d))], gb.at[h], gs.at[d - 1], gr.at[d - 1], (dp, hh(d))))
    sent += cq
    locals_ = [
        pltpu.make_async_copy(q_ref.at[0, :, cols(h)], qb.at[h], loc.at[0]),
        pltpu.make_async_copy(g_ref.at[0, :, cols(h)], gb.at[h], loc.at[1]),
        pltpu.make_async_copy(p_ref.at[z, par, half], own, loc.at[2]),
    ]
    for copy in locals_:
        copy.start()

    c2 = {}

    def forward_y(dz):
        for dy in E_ORDER:
            src = p_ref.at[z, par, yy(dy) // 2] if dz == 0 else i1.at[dz - 1, yy(dy) // 2]
            i = dy // 2 - 1
            c2[dy, dz] = remote(src, fin.at[i, dz], s2ys.at[i, dz], s2yr.at[i, dz], at(0, dy))
            sent.append(c2[dy, dz])

    def forward_z(dy):
        i = dy // 2
        for dz in Z_ORDER:
            c2[dy, dz] = remote(i2.at[i, zz(dz)], fin.at[3 + i, dz], s2zs.at[i, dz - 1], s2zr.at[i, dz - 1], at(dz, 0))
            sent.append(c2[dy, dz])

    forward_y(0)

    for copy in locals_:
        copy.wait()
    for copy in cq:
        copy.wait_recv()
    length = len_ref[dp]
    limit = tiles_ref[dp] * TILE
    row_live = lax.broadcasted_iota(jnp.int32, (N * 16, HD), 0) < length
    q_gain = qg_ref[...] * (HD ** -0.5)

    def raw(ref, g):
        return ref[:, :, g * HD:(g + 1) * HD].reshape(N * 16, HD).astype(jnp.float32)

    for g in range(GQ):
        here = slice(g * N * 16, (g + 1) * N * 16)
        q = raw(qb, g)
        mean_sq = jnp.mean(q * q, axis=-1, keepdims=True)
        qn[here, :] = (q * lax.rsqrt(mean_sq + EPSILON) * q_gain).astype(jnp.bfloat16)
        gm[here, :] = jnp.where(row_live, raw(gb, g), 0.0).astype(jnp.bfloat16)
    for ref in (acc_a, acc_b, acc_c, acc_t):
        ref[...] = jnp.zeros_like(ref)

    for kind, d in order:
        c1[kind, d].wait_recv()
        if kind == "z":
            forward_y(d)
        else:
            forward_z(d)

    k_gain = kg_ref[...]
    width_b = N * ROWS
    lane = lax.broadcasted_iota(jnp.int32, (1, width_b), 1)
    lane_dz = lane // ROWS
    lane_j = lane % ROWS

    def block(dy):
        chunks = []
        for dz in range(N):
            if dy == 0:
                chunks.append(own[...] if dz == 0 else i1[dz - 1, half])
            elif dy % 2 == 0:
                c2[dy, dz].wait_recv()
                chunks.append(fin[dy // 2 - 1, dz])
            elif dz == 0:
                chunks.append(i2[dy // 2, z])
            else:
                c2[dy, dz].wait_recv()
                chunks.append(fin[3 + dy // 2, dz])
        for i in range(0, N, 2):
            both = jnp.concatenate([chunks[i].astype(jnp.float32), chunks[i + 1].astype(jnp.float32)], axis=0)
            k = both[:, :HD]
            mean_sq = jnp.mean(k * k, axis=-1, keepdims=True)
            k = k * lax.rsqrt(mean_sq + EPSILON) * k_gain
            vk[i * ROWS:(i + 2) * ROWS, :HD] = both[:, HD:].astype(jnp.bfloat16)
            vk[i * ROWS:(i + 2) * ROWS, HD:] = k.astype(jnp.bfloat16)
        source = ((z - lane_dz + N) % N) * N + (y - dy + N) % N
        live = ((lane_j < slots) & (source * slots + lane_j < limit)).astype(jnp.float32)

        def rows(r, carry):
            here = pl.ds(pl.multiple_of(r * GROUP, GROUP), GROUP)
            q, g = qn[here, :], gm[here, :]
            a, t = acc_a[here, :], acc_t[here, :]
            s = lax.dot_general(q, vk[:, HD:], NT, preferred_element_type=jnp.float32)
            w = (jnp.exp(s) * live).astype(jnp.bfloat16)
            pg = lax.dot_general(g, vk[:, :HD], NT, preferred_element_type=jnp.float32)
            wf = w.astype(jnp.float32)
            ac = jnp.dot(w, vk[...], preferred_element_type=jnp.float32)
            a_now = a + ac[:, :HD]
            t_now = t + jnp.sum(wf, axis=-1, keepdims=True)
            if dy == 0:
                a, t = a_now, t_now
            d0 = jnp.sum(g.astype(jnp.float32) * a, axis=-1, keepdims=True) / jnp.maximum(t[:, :1], 1e-30)
            p = (wf * (pg - d0)).astype(jnp.bfloat16)
            b = jnp.dot(p, vk[:, HD:], preferred_element_type=jnp.float32)
            acc_a[here, :] = a_now
            acc_t[here, :] = t_now
            acc_b[here, :] = acc_b[here, :] + b + d0 * ac[:, HD:]
            acc_c[here, :] = acc_c[here, :] + ac[:, HD:]
            return carry

        lax.fori_loop(0, N * 16 * GQ // GROUP, rows, 0, unroll=True)

    for dy in BLOCK_ORDER:
        block(dy)

    for g in range(GQ):
        here = slice(g * N * 16, (g + 1) * N * 16)
        there = slice(g * HD, (g + 1) * HD)
        t = acc_t[here, :]
        att = jnp.where(row_live, acc_a[here, :] / t, 0.0)
        ao[:, :, there] = att.astype(jnp.bfloat16).reshape(N, 16, HD)
        delta = jnp.sum(gm[here, :].astype(jnp.float32) * att, axis=-1, keepdims=True)
        norm_grad = (acc_b[here, :] - delta * acc_c[here, :]) / t
        q = raw(qb, g)
        r = lax.rsqrt(jnp.mean(q * q, axis=-1, keepdims=True) + EPSILON)
        u = norm_grad * q_gain
        dq = r * u - q * (r * r * r * jnp.mean(q * u, axis=-1, keepdims=True))
        go[:, :, there] = dq.astype(jnp.bfloat16).reshape(N, 16, HD)
    outs = []
    for d in range(1, N):
        outs.append(remote(ao.at[hh(d)], att_ref.at[0, :, cols(h)], oas.at[d - 1], oar.at[d - 1], (dp, hh(d))))
        outs.append(remote(go.at[hh(d)], grad_ref.at[0, :, cols(h)], ogs.at[d - 1], ogr.at[d - 1], (dp, hh(d))))
    mine = [
        pltpu.make_async_copy(ao.at[h], att_ref.at[0, :, cols(h)], loc.at[0]),
        pltpu.make_async_copy(go.at[h], grad_ref.at[0, :, cols(h)], loc.at[1]),
    ]
    for copy in mine:
        copy.start()
    for copy in sent:
        copy.wait_send()
    for copy in mine:
        copy.wait()
    for copy in outs:
        copy.wait()


def local(queries, out_grad, q_gain, k_gain, image_keys, image_values, image_tiles, text_len):
    samples, slots, _ = image_keys.shape
    both = jnp.concatenate([image_keys, image_values], axis=-1)
    both = jnp.pad(both, ((0, 0), (0, ROWS - slots), (0, 0)))
    packed = both.reshape(N, N // 2, 2, ROWS, 2 * HD).transpose(0, 2, 1, 3, 4)
    rows = queries.shape[1] * N
    q_rows = rows * GQ
    bf, f32 = jnp.bfloat16, jnp.float32
    dma = pltpu.SemaphoreType.DMA
    vmem = pl.BlockSpec(memory_space=pltpu.VMEM)
    smem = pl.BlockSpec(memory_space=pltpu.SMEM)
    hbm = pl.BlockSpec(memory_space=pl.ANY)
    out = jax.ShapeDtypeStruct(queries.shape, bf)

    return tuple(pl.pallas_call(
        functools.partial(kernel, slots),
        name="exchange_attention",
        out_shape=(out, out),
        in_specs=[smem, smem, hbm, hbm, vmem, vmem, hbm],
        out_specs=(hbm, hbm),
        scratch_shapes=[
            pltpu.VMEM((N, 16, GQ * HD), bf),
            pltpu.VMEM((N, 16, GQ * HD), bf),
            pltpu.VMEM((7, 4, ROWS, 2 * HD), bf),
            pltpu.VMEM((4, N, ROWS, 2 * HD), bf),
            pltpu.VMEM((7, N, ROWS, 2 * HD), bf),
            pltpu.VMEM((ROWS, 2 * HD), bf),
            pltpu.VMEM((N * ROWS, 2 * HD), bf),
            pltpu.VMEM((q_rows, HD), bf),
            pltpu.VMEM((q_rows, HD), bf),
            pltpu.VMEM((q_rows, HD), f32),
            pltpu.VMEM((q_rows, HD), f32),
            pltpu.VMEM((q_rows, HD), f32),
            pltpu.VMEM((q_rows, HD), f32),
            pltpu.VMEM((N, 16, GQ * HD), bf),
            pltpu.VMEM((N, 16, GQ * HD), bf),
            dma((7,)), dma((7,)), dma((7,)), dma((7,)),
            dma((7,)), dma((7,)), dma((4,)), dma((4,)),
            dma((3, N)), dma((3, N)), dma((4, 7)), dma((4, 7)),
            dma((7,)), dma((7,)), dma((7,)), dma((7,)),
            dma((3,)),
        ],
        compiler_params=pltpu.CompilerParams(
            collective_id=0, has_side_effects=True, vmem_limit_bytes=48 * 2 ** 20),
        cost_estimate=pl.CostEstimate(flops=8_000_000_000, bytes_accessed=8_000_000, transcendentals=7_000_000),
    )(image_tiles, text_len, queries, out_grad, q_gain.reshape(1, HD), k_gain.reshape(1, HD), packed))


def solution(mesh):
    return jax.shard_map(
        local,
        mesh=mesh,
        in_specs=(
            P("dp", "heads", None),
            P("dp", "heads", None),
            P(),
            P(),
            P(None, "dp", "heads"),
            P(None, "dp", "heads"),
            P(),
            P(),
        ),
        out_specs=(P("dp", "heads", None), P("dp", "heads", None)),
        check_vma=False,
    )
```

```python
import functools

import jax
import jax.numpy as jnp
from jax import lax
from jax.experimental import pallas as pl
from jax.experimental.pallas import tpu as pltpu
from jax.sharding import PartitionSpec as P

MESH = pl.DeviceIdType.MESH
EPSILON = 1e-05
TILE = 1601
HD = 128
GQ = 8
ROWS = 104
N = 8
SLABS = (1, 7, 2, 6, 3, 5, 4, 0)
READY = 2
FINAL = 2
PLAN = (
    ("send", 1), ("send", 7), ("send", 2), ("send", 6), ("rows", 0),
    ("forward", 1), ("forward", 7), ("send", 3), ("send", 5), ("send", 4),
    ("forward", 2), ("forward", 6), ("send", 0), ("attend", 1), ("attend", 7),
    ("forward", 3), ("forward", 5), ("attend", 2), ("attend", 6), ("forward", 4),
    ("attend", 3), ("attend", 5), ("attend", 0), ("attend", 4),
)
ODD = (1, 7, 3, 5)
EVEN = (2, 6, 4)
PARTS = 2
NT = (((1,), (1,)), ((), ()))
GROUP = 256


def kernel(slots, tiles_ref, len_ref, q_ref, g_ref, qg_ref, kg_ref, k_ref, v_ref, att_ref, grad_ref,
           kin, vin, pk, qb, gb, i1, i2, fin, vk, qn, gm, acc_a, acc_b, acc_c, acc_t, ao, go,
           qs, qr, gs, gr, s1zs, s1zr, s1ys, s1yr, s2ys, s2yr, s2zs, s2zr, oas, oar, ogs, ogr, kin_sem, vin_sem, loc):
    dp = lax.axis_index("dp")
    h = lax.axis_index("heads")
    z, y = dp // N, dp % N
    par, half = y % 2, y // 2

    def zz(d):
        return (z + d) % N

    def yy(d):
        return (y + d) % N

    def at(dz, dy):
        return (zz(dz) * N + yy(dy), h)

    def hh(d):
        return (h + d) % N

    def remote(src, dst, ssem, rsem, dev):
        copy = pltpu.make_async_remote_copy(
            src_ref=src, dst_ref=dst, send_sem=ssem, recv_sem=rsem, device_id=dev, device_id_type=MESH)
        copy.start()
        return copy

    width = GQ * HD

    def cols(i, part=0, parts=1):
        return pl.ds(pl.multiple_of(i * width + part * (width // parts), width // parts), width // parts)

    loads = {}
    for d in SLABS:
        loads[d] = (pltpu.make_async_copy(k_ref.at[:, zz(d)], kin.at[d], kin_sem.at[d]),
                    pltpu.make_async_copy(v_ref.at[:, zz(d)], vin.at[d], vin_sem.at[d]))
        for copy in loads[d]:
            copy.start()
    own = [
        pltpu.make_async_copy(q_ref.at[0, :, cols(h)], qb.at[h], loc.at[0]),
        pltpu.make_async_copy(g_ref.at[0, :, cols(h)], gb.at[h], loc.at[1]),
    ]
    for copy in own:
        copy.start()

    barrier = pltpu.get_barrier_semaphore()
    for d in range(1, N):
        for dev in (at(d, 0), at(0, d), (dp, hh(d))):
            pl.semaphore_signal(barrier, inc=1, device_id=dev, device_id_type=MESH)

    def pack(d):
        for copy in loads[d]:
            copy.wait()
        for ref, lanes in ((kin, slice(0, HD)), (vin, slice(HD, 2 * HD))):
            x = ref[d].astype(jnp.float32)
            x = jnp.concatenate([x, jnp.zeros((ROWS - slots,) + x.shape[1:], jnp.float32)], axis=0)
            x = jnp.swapaxes(x, 0, 1).astype(jnp.bfloat16)
            for i in range(N):
                pk[zz(d), i % 2, i // 2, :, lanes] = x[i]

    for d in SLABS[:READY]:
        pack(d)
    pl.semaphore_wait(barrier, 3 * (N - 1))

    sent = []
    cq = []
    for d in range(1, N):
        cq.append(remote(q_ref.at[0, :, cols(hh(d))], qb.at[h], qs.at[d - 1], qr.at[d - 1], (dp, hh(d))))
        cq.append(remote(g_ref.at[0, :, cols(hh(d))], gb.at[h], gs.at[d - 1], gr.at[d - 1], (dp, hh(d))))
    sent += cq

    c1z, c1y, c2 = {}, {}, {}

    def forward_y(dz):
        for dy in EVEN:
            src = pk.at[z, par, yy(dy) // 2] if dz == 0 else i1.at[dz - 1, yy(dy) // 2]
            i = dy // 2 - 1
            c2[dy, dz] = remote(src, fin.at[i, dz], s2ys.at[i, dz], s2yr.at[i, dz], at(0, dy))
            sent.append(c2[dy, dz])

    def forward_z(dy, dz):
        i = dy // 2
        c2[dy, dz] = remote(i2.at[i, zz(dz)], fin.at[3 + i, dz], s2zs.at[i, dz - 1], s2zr.at[i, dz - 1], at(dz, 0))
        sent.append(c2[dy, dz])

    def send(d):
        if d not in SLABS[:READY]:
            pack(d)
        if d:
            c1z[d] = remote(pk.at[zz(d), par], i1.at[d - 1], s1zs.at[d - 1], s1zr.at[d - 1], at(d, 0))
            sent.append(c1z[d])
        for dy in ODD:
            i = dy // 2
            c1y[dy, d] = remote(pk.at[zz(d), yy(dy) % 2, yy(dy) // 2], i2.at[i, zz(d)], s1ys.at[i, d], s1yr.at[i, d], at(0, dy))
            sent.append(c1y[dy, d])
        if d == 0:
            forward_y(0)

    def forward(d):
        c1z[d].wait_recv()
        forward_y(d)
        for dy in ODD:
            c1y[dy, d].wait_recv()
            forward_z(dy, d)

    length = len_ref[dp]
    limit = tiles_ref[dp] * TILE
    row_live = lax.broadcasted_iota(jnp.int32, (N * 16, HD), 0) < length
    q_gain = qg_ref[...] * (HD ** -0.5)

    def raw(ref, g):
        return ref[:, :, g * HD:(g + 1) * HD].reshape(N * 16, HD).astype(jnp.float32)

    def stage_rows():
        for copy in own:
            copy.wait()
        for copy in cq:
            copy.wait_recv()
        for g in range(GQ):
            here = slice(g * N * 16, (g + 1) * N * 16)
            q = raw(qb, g)
            mean_sq = jnp.mean(q * q, axis=-1, keepdims=True)
            qn[here, :] = (q * lax.rsqrt(mean_sq + EPSILON) * q_gain).astype(jnp.bfloat16)
            gm[here, :] = jnp.where(row_live, raw(gb, g), 0.0).astype(jnp.bfloat16)
        for ref in (acc_a, acc_b, acc_c, acc_t):
            ref[...] = jnp.zeros_like(ref)

    k_gain = kg_ref[...]
    width_b = N * ROWS
    lane = lax.broadcasted_iota(jnp.int32, (1, width_b), 1)
    lane_dy = lane // ROWS
    lane_j = lane % ROWS

    def stage(dz, slot=0):
        chunks = []
        for dy in range(N):
            if dz == 0 and dy % 2:
                c1y[dy, 0].wait_recv()
                chunks.append(i2[dy // 2, z])
            elif dy == 0:
                chunks.append(i1[dz - 1, half] if dz else pk[z, par, half])
            else:
                c2[dy, dz].wait_recv()
                chunks.append(fin[3 + dy // 2 if dy % 2 else dy // 2 - 1, dz])
        for i in range(0, N, 2):
            both = jnp.concatenate([chunks[i].astype(jnp.float32), chunks[i + 1].astype(jnp.float32)], axis=0)
            k = both[:, :HD]
            mean_sq = jnp.mean(k * k, axis=-1, keepdims=True)
            k = k * lax.rsqrt(mean_sq + EPSILON) * k_gain
            vk[slot, i * ROWS:(i + 2) * ROWS, :HD] = both[:, HD:].astype(jnp.bfloat16)
            vk[slot, i * ROWS:(i + 2) * ROWS, HD:] = k.astype(jnp.bfloat16)
        source = (z - dz + N) % N * N + (y - lane_dy + N) % N
        return ((lane_j < slots) & (source * slots + lane_j < limit)).astype(jnp.float32)

    def attend(live, first, last, shift_now, slot=0):
        def rows(r, carry):
            here = pl.ds(pl.multiple_of(r * GROUP, GROUP), GROUP)
            q, g = qn[here, :], gm[here, :]
            a, t = acc_a[here, :], acc_t[here, :]
            s = lax.dot_general(q, vk[slot, :, HD:], NT, preferred_element_type=jnp.float32)
            w = (jnp.exp(s) * live).astype(jnp.bfloat16)
            pg = lax.dot_general(g, vk[slot, :, :HD], NT, preferred_element_type=jnp.float32)
            wf = w.astype(jnp.float32)
            ac = jnp.dot(w, vk[slot], preferred_element_type=jnp.float32)
            a_now = a + ac[:, :HD]
            t_now = t + jnp.sum(wf, axis=-1, keepdims=True)
            if shift_now:
                a, t = a_now, t_now
            d0 = jnp.sum(g.astype(jnp.float32) * a, axis=-1, keepdims=True) / jnp.maximum(t[:, :1], 1e-30)
            p = (wf * (pg - d0)).astype(jnp.bfloat16)
            b = jnp.dot(p, vk[slot, :, HD:], preferred_element_type=jnp.float32)
            acc_a[here, :] = a_now
            acc_t[here, :] = t_now
            acc_b[here, :] = acc_b[here, :] + b + d0 * ac[:, HD:]
            acc_c[here, :] = acc_c[here, :] + ac[:, HD:]
            return carry

        lax.fori_loop(first, last, rows, 0, unroll=True)

    outs = []

    def finish(part):
        heads = GQ // PARTS
        for g in range(part * heads, (part + 1) * heads):
            here = slice(g * N * 16, (g + 1) * N * 16)
            there = slice(g * HD, (g + 1) * HD)
            t = acc_t[here, :]
            att = jnp.where(row_live, acc_a[here, :] / t, 0.0)
            ao[:, :, there] = att.astype(jnp.bfloat16).reshape(N, 16, HD)
            delta = jnp.sum(gm[here, :].astype(jnp.float32) * att, axis=-1, keepdims=True)
            norm_grad = (acc_b[here, :] - delta * acc_c[here, :]) / t
            q = raw(qb, g)
            r = lax.rsqrt(jnp.mean(q * q, axis=-1, keepdims=True) + EPSILON)
            u = norm_grad * q_gain
            dq = r * u - q * (r * r * r * jnp.mean(q * u, axis=-1, keepdims=True))
            go[:, :, there] = dq.astype(jnp.bfloat16).reshape(N, 16, HD)
        mine = pl.ds(part * heads * HD, heads * HD)
        for i, (buf, ref, ssem, rsem) in enumerate(((ao, att_ref, oas, oar), (go, grad_ref, ogs, ogr))):
            target = ref.at[0, :, cols(h, part, PARTS)]
            for d in range(1, N):
                outs.append(remote(buf.at[hh(d), :, mine], target, ssem.at[part, d - 1], rsem.at[part, d - 1], (dp, hh(d))))
            copy = pltpu.make_async_copy(buf.at[h, :, mine], target, loc.at[2 + 2 * part + i])
            copy.start()
            outs.append(copy)

    groups = N * 16 * GQ // GROUP
    attended = []
    for what, d in PLAN:
        if what == "send":
            send(d)
        elif what == "rows":
            stage_rows()
        elif what == "forward":
            forward(d)
        else:
            attended.append(d)
            if len(attended) + FINAL <= N:
                attend(stage(d), 0, groups, len(attended) <= 6)
    lives = {}
    for part in range(PARTS):
        for slot, d in enumerate(attended[N - FINAL:]):
            if part == 0:
                lives[d] = stage(d, slot)
            attend(lives[d], part * groups // PARTS, (part + 1) * groups // PARTS, False, slot)
        finish(part)
    for copy in sent:
        copy.wait_send()
    for copy in outs:
        copy.wait()


def place(a_ref, b_ref, x_ref, y_ref):
    x_ref[...] = a_ref[...]
    y_ref[...] = b_ref[...]


def local(queries, out_grad, q_gain, k_gain, image_keys, image_values, image_tiles, text_len):
    samples, slots, _ = image_keys.shape
    keys = image_keys.transpose(1, 0, 2).reshape(slots, N, N, HD)
    values = image_values.transpose(1, 0, 2).reshape(slots, N, N, HD)
    rows = queries.shape[1] * N
    q_rows = rows * GQ
    bf, f32 = jnp.bfloat16, jnp.float32
    dma = pltpu.SemaphoreType.DMA
    vmem = pl.BlockSpec(memory_space=pltpu.VMEM)
    smem = pl.BlockSpec(memory_space=pltpu.SMEM)
    hbm = pl.BlockSpec(memory_space=pl.ANY)
    out = jax.ShapeDtypeStruct(queries.shape, bf)

    attention, query_grad = pl.pallas_call(
        functools.partial(kernel, slots),
        name="exchange_attention",
        out_shape=(out, out),
        in_specs=[smem, smem, hbm, hbm, vmem, vmem, hbm, hbm],
        out_specs=(hbm, hbm),
        scratch_shapes=[
            pltpu.VMEM((N, slots, N, HD), bf),
            pltpu.VMEM((N, slots, N, HD), bf),
            pltpu.VMEM((N, 2, N // 2, ROWS, 2 * HD), bf),
            pltpu.VMEM((N, 16, GQ * HD), bf),
            pltpu.VMEM((N, 16, GQ * HD), bf),
            pltpu.VMEM((7, 4, ROWS, 2 * HD), bf),
            pltpu.VMEM((4, N, ROWS, 2 * HD), bf),
            pltpu.VMEM((7, N, ROWS, 2 * HD), bf),
            pltpu.VMEM((FINAL, N * ROWS, 2 * HD), bf),
            pltpu.VMEM((q_rows, HD), bf),
            pltpu.VMEM((q_rows, HD), bf),
            pltpu.VMEM((q_rows, HD), f32),
            pltpu.VMEM((q_rows, HD), f32),
            pltpu.VMEM((q_rows, HD), f32),
            pltpu.VMEM((q_rows, HD), f32),
            pltpu.VMEM((N, 16, GQ * HD), bf),
            pltpu.VMEM((N, 16, GQ * HD), bf),
            dma((7,)), dma((7,)), dma((7,)), dma((7,)),
            dma((7,)), dma((7,)), dma((4, N)), dma((4, N)),
            dma((3, N)), dma((3, N)), dma((4, 7)), dma((4, 7)),
            dma((PARTS, 7)), dma((PARTS, 7)), dma((PARTS, 7)), dma((PARTS, 7)),
            dma((N,)), dma((N,)), dma((2 + 2 * PARTS,)),
        ],
        compiler_params=pltpu.CompilerParams(
            collective_id=0, has_side_effects=True, vmem_limit_bytes=60 * 2 ** 20),
        cost_estimate=pl.CostEstimate(flops=8_000_000_000, bytes_accessed=8_000_000, transcendentals=7_000_000),
    )(image_tiles, text_len, queries, out_grad, q_gain.reshape(1, HD), k_gain.reshape(1, HD), keys, values)

    return tuple(pl.pallas_call(
        place,
        name="place_results",
        out_shape=(out, out),
        in_specs=[vmem, vmem],
        out_specs=(vmem, vmem),
        compiler_params=pltpu.CompilerParams(vmem_limit_bytes=60 * 2 ** 20),
    )(attention, query_grad))


def solution(mesh):
    return jax.shard_map(
        local,
        mesh=mesh,
        in_specs=(
            P("dp", "heads", None),
            P("dp", "heads", None),
            P(),
            P(),
            P(None, "dp", "heads"),
            P(None, "dp", "heads"),
            P(),
            P(),
        ),
        out_specs=(P("dp", "heads", None), P("dp", "heads", None)),
        check_vma=False,
    )
```

```python
import functools

import jax
import jax.numpy as jnp
from jax import lax
from jax.experimental import pallas as pl
from jax.experimental.pallas import tpu as pltpu
from jax.sharding import PartitionSpec as P

MESH = pl.DeviceIdType.MESH
EPSILON = 1e-05
TILE = 1601
HD = 128
GQ = 8
ROWS = 104
N = 8
SLABS = (1, 7, 2, 6, 0, 3, 5, 4)
READY = 2
FINAL = 2
PLAN = (
    ("send", 1), ("send", 7), ("rows", 0), ("send", 2), ("send", 6), ("send", 0),
    ("forward", 1), ("forward", 7), ("send", 3), ("send", 5), ("send", 4), ("norm", 0),
    ("forward", 2), ("forward", 6), ("attend", 0), ("attend", 1), ("forward", 3), ("attend", 7),
    ("forward", 5), ("attend", 2), ("forward", 4), ("attend", 6), ("attend", 3), ("attend", 5),
    ("attend", 4),
)
ODD = (1, 7, 3, 5)
EVEN = (2, 6, 4)
PARTS = 2
NT = (((1,), (1,)), ((), ()))
GROUP = 256


def kernel(slots, tiles_ref, len_ref, q_ref, g_ref, qg_ref, kg_ref, k_ref, v_ref, att_ref, grad_ref,
           kin, vin, pk, qb, gb, i1, i2, fin, vk, qn, gm, acc_a, acc_b, acc_c, acc_t, ao, go,
           qs, qr, gs, gr, s1zs, s1zr, s1ys, s1yr, s2ys, s2yr, s2zs, s2zr, oas, oar, ogs, ogr, kin_sem, vin_sem, loc):
    dp = lax.axis_index("dp")
    h = lax.axis_index("heads")
    z, y = dp // N, dp % N
    par, half = y % 2, y // 2

    def zz(d):
        return (z + d) % N

    def yy(d):
        return (y + d) % N

    def at(dz, dy):
        return (zz(dz) * N + yy(dy), h)

    def hh(d):
        return (h + d) % N

    def remote(src, dst, ssem, rsem, dev):
        copy = pltpu.make_async_remote_copy(
            src_ref=src, dst_ref=dst, send_sem=ssem, recv_sem=rsem, device_id=dev, device_id_type=MESH)
        copy.start()
        return copy

    width = GQ * HD

    def cols(i, part=0, parts=1):
        return pl.ds(pl.multiple_of(i * width + part * (width // parts), width // parts), width // parts)

    loads = {}
    for d in SLABS:
        loads[d] = (pltpu.make_async_copy(k_ref.at[:, zz(d)], kin.at[d], kin_sem.at[d]),
                    pltpu.make_async_copy(v_ref.at[:, zz(d)], vin.at[d], vin_sem.at[d]))
        for copy in loads[d]:
            copy.start()
    own = [
        pltpu.make_async_copy(q_ref.at[0, :, cols(h)], qb.at[h], loc.at[0]),
        pltpu.make_async_copy(g_ref.at[0, :, cols(h)], gb.at[h], loc.at[1]),
    ]
    for copy in own:
        copy.start()

    barrier = pltpu.get_barrier_semaphore()
    for d in range(1, N):
        for dev in (at(d, 0), at(0, d), (dp, hh(d))):
            pl.semaphore_signal(barrier, inc=1, device_id=dev, device_id_type=MESH)

    def pack(d):
        for copy in loads[d]:
            copy.wait()
        for ref, lanes in ((kin, slice(0, HD)), (vin, slice(HD, 2 * HD))):
            x = ref[d].astype(jnp.float32)
            x = jnp.concatenate([x, jnp.zeros((ROWS - slots,) + x.shape[1:], jnp.float32)], axis=0)
            x = jnp.swapaxes(x, 0, 1).astype(jnp.bfloat16)
            for i in range(N):
                pk[zz(d), i % 2, i // 2, :, lanes] = x[i]

    for d in SLABS[:READY]:
        pack(d)
    pl.semaphore_wait(barrier, 3 * (N - 1))

    sent = []
    cq = []

    def send_rows():
        for d in range(1, N):
            cq.append(remote(q_ref.at[0, :, cols(hh(d))], qb.at[h], qs.at[d - 1], qr.at[d - 1], (dp, hh(d))))
            cq.append(remote(g_ref.at[0, :, cols(hh(d))], gb.at[h], gs.at[d - 1], gr.at[d - 1], (dp, hh(d))))
        sent.extend(cq)


    c1z, c1y, c2 = {}, {}, {}

    def forward_y(dz):
        for dy in EVEN:
            src = pk.at[z, par, yy(dy) // 2] if dz == 0 else i1.at[dz - 1, yy(dy) // 2]
            i = dy // 2 - 1
            c2[dy, dz] = remote(src, fin.at[i, dz], s2ys.at[i, dz], s2yr.at[i, dz], at(0, dy))
            sent.append(c2[dy, dz])

    def forward_z(dy, dz):
        i = dy // 2
        c2[dy, dz] = remote(i2.at[i, zz(dz)], fin.at[3 + i, dz], s2zs.at[i, dz - 1], s2zr.at[i, dz - 1], at(dz, 0))
        sent.append(c2[dy, dz])

    def send(d):
        if d not in SLABS[:READY]:
            pack(d)
        if d:
            c1z[d] = remote(pk.at[zz(d), par], i1.at[d - 1], s1zs.at[d - 1], s1zr.at[d - 1], at(d, 0))
            sent.append(c1z[d])
        for dy in ODD:
            i = dy // 2
            c1y[dy, d] = remote(pk.at[zz(d), yy(dy) % 2, yy(dy) // 2], i2.at[i, zz(d)], s1ys.at[i, d], s1yr.at[i, d], at(0, dy))
            sent.append(c1y[dy, d])
        if d == 0:
            forward_y(0)

    def forward(d):
        c1z[d].wait_recv()
        forward_y(d)
        for dy in ODD:
            c1y[dy, d].wait_recv()
            forward_z(dy, d)

    length = len_ref[dp]
    limit = tiles_ref[dp] * TILE
    row_live = lax.broadcasted_iota(jnp.int32, (N * 16, HD), 0) < length
    q_gain = qg_ref[...] * (HD ** -0.5)

    def raw(ref, g):
        return ref[:, :, g * HD:(g + 1) * HD].reshape(N * 16, HD).astype(jnp.float32)

    def stage_rows():
        for copy in own:
            copy.wait()
        for copy in cq:
            copy.wait_recv()
        for g in range(GQ):
            here = slice(g * N * 16, (g + 1) * N * 16)
            q = raw(qb, g)
            mean_sq = jnp.mean(q * q, axis=-1, keepdims=True)
            qn[here, :] = (q * lax.rsqrt(mean_sq + EPSILON) * q_gain).astype(jnp.bfloat16)
            gm[here, :] = jnp.where(row_live, raw(gb, g), 0.0).astype(jnp.bfloat16)
        for ref in (acc_a, acc_b, acc_c, acc_t):
            ref[...] = jnp.zeros_like(ref)

    k_gain = kg_ref[...]
    width_b = N * ROWS
    lane = lax.broadcasted_iota(jnp.int32, (1, width_b), 1)
    lane_dy = lane // ROWS
    lane_j = lane % ROWS

    def stage(dz, slot=0):
        chunks = []
        for dy in range(N):
            if dz == 0 and dy % 2:
                c1y[dy, 0].wait_recv()
                chunks.append(i2[dy // 2, z])
            elif dy == 0:
                chunks.append(i1[dz - 1, half] if dz else pk[z, par, half])
            else:
                c2[dy, dz].wait_recv()
                chunks.append(fin[3 + dy // 2 if dy % 2 else dy // 2 - 1, dz])
        for i in range(0, N, 2):
            both = jnp.concatenate([chunks[i].astype(jnp.float32), chunks[i + 1].astype(jnp.float32)], axis=0)
            k = both[:, :HD]
            mean_sq = jnp.mean(k * k, axis=-1, keepdims=True)
            k = k * lax.rsqrt(mean_sq + EPSILON) * k_gain
            vk[slot, i * ROWS:(i + 2) * ROWS, :HD] = both[:, HD:].astype(jnp.bfloat16)
            vk[slot, i * ROWS:(i + 2) * ROWS, HD:] = k.astype(jnp.bfloat16)
        source = (z - dz + N) % N * N + (y - lane_dy + N) % N
        return ((lane_j < slots) & (source * slots + lane_j < limit)).astype(jnp.float32)

    def attend(live, first, last, shift_now, slot=0):
        def rows(r, carry):
            here = pl.ds(pl.multiple_of(r * GROUP, GROUP), GROUP)
            q, g = qn[here, :], gm[here, :]
            a, t = acc_a[here, :], acc_t[here, :]
            s = lax.dot_general(q, vk[slot, :, HD:], NT, preferred_element_type=jnp.float32)
            w = (jnp.exp(s) * live).astype(jnp.bfloat16)
            pg = lax.dot_general(g, vk[slot, :, :HD], NT, preferred_element_type=jnp.float32)
            wf = w.astype(jnp.float32)
            ac = jnp.dot(w, vk[slot], preferred_element_type=jnp.float32)
            a_now = a + ac[:, :HD]
            t_now = t + jnp.sum(wf, axis=-1, keepdims=True)
            if shift_now:
                a, t = a_now, t_now
            d0 = jnp.sum(g.astype(jnp.float32) * a, axis=-1, keepdims=True) / jnp.maximum(t[:, :1], 1e-30)
            p = (wf * (pg - d0)).astype(jnp.bfloat16)
            b = jnp.dot(p, vk[slot, :, HD:], preferred_element_type=jnp.float32)
            acc_a[here, :] = a_now
            acc_t[here, :] = t_now
            acc_b[here, :] = acc_b[here, :] + b + d0 * ac[:, HD:]
            acc_c[here, :] = acc_c[here, :] + ac[:, HD:]
            return carry

        lax.fori_loop(first, last, rows, 0, unroll=True)

    outs = []

    def finish(part):
        heads = GQ // PARTS
        for g in range(part * heads, (part + 1) * heads):
            here = slice(g * N * 16, (g + 1) * N * 16)
            there = slice(g * HD, (g + 1) * HD)
            t = acc_t[here, :]
            att = jnp.where(row_live, acc_a[here, :] / t, 0.0)
            ao[:, :, there] = att.astype(jnp.bfloat16).reshape(N, 16, HD)
            delta = jnp.sum(gm[here, :].astype(jnp.float32) * att, axis=-1, keepdims=True)
            norm_grad = (acc_b[here, :] - delta * acc_c[here, :]) / t
            q = raw(qb, g)
            r = lax.rsqrt(jnp.mean(q * q, axis=-1, keepdims=True) + EPSILON)
            u = norm_grad * q_gain
            dq = r * u - q * (r * r * r * jnp.mean(q * u, axis=-1, keepdims=True))
            go[:, :, there] = dq.astype(jnp.bfloat16).reshape(N, 16, HD)
        mine = pl.ds(part * heads * HD, heads * HD)
        for i, (buf, ref, ssem, rsem) in enumerate(((ao, att_ref, oas, oar), (go, grad_ref, ogs, ogr))):
            target = ref.at[0, :, cols(h, part, PARTS)]
            for d in range(1, N):
                outs.append(remote(buf.at[hh(d), :, mine], target, ssem.at[part, d - 1], rsem.at[part, d - 1], (dp, hh(d))))
            copy = pltpu.make_async_copy(buf.at[h, :, mine], target, loc.at[2 + 2 * part + i])
            copy.start()
            outs.append(copy)

    groups = N * 16 * GQ // GROUP
    attended = []
    for what, d in PLAN:
        if what == "send":
            send(d)
        elif what == "rows":
            send_rows()
        elif what == "norm":
            stage_rows()
        elif what == "forward":
            forward(d)
        else:
            attended.append(d)
            if len(attended) + FINAL <= N:
                attend(stage(d), 0, groups, len(attended) <= 6)
    lives = {}
    for part in range(PARTS):
        for slot, d in enumerate(attended[N - FINAL:]):
            if part == 0:
                lives[d] = stage(d, slot)
            attend(lives[d], part * groups // PARTS, (part + 1) * groups // PARTS, slot + 1 < FINAL, slot)
        finish(part)
    for copy in sent:
        copy.wait_send()
    for copy in outs:
        copy.wait()


def place(a_ref, b_ref, x_ref, y_ref):
    x_ref[...] = a_ref[...]
    y_ref[...] = b_ref[...]


def local(queries, out_grad, q_gain, k_gain, image_keys, image_values, image_tiles, text_len):
    samples, slots, _ = image_keys.shape
    keys = image_keys.transpose(1, 0, 2).reshape(slots, N, N, HD)
    values = image_values.transpose(1, 0, 2).reshape(slots, N, N, HD)
    rows = queries.shape[1] * N
    q_rows = rows * GQ
    bf, f32 = jnp.bfloat16, jnp.float32
    dma = pltpu.SemaphoreType.DMA
    vmem = pl.BlockSpec(memory_space=pltpu.VMEM)
    smem = pl.BlockSpec(memory_space=pltpu.SMEM)
    hbm = pl.BlockSpec(memory_space=pl.ANY)
    out = jax.ShapeDtypeStruct(queries.shape, bf)

    attention, query_grad = pl.pallas_call(
        functools.partial(kernel, slots),
        name="exchange_attention",
        out_shape=(out, out),
        in_specs=[smem, smem, hbm, hbm, vmem, vmem, hbm, hbm],
        out_specs=(hbm, hbm),
        scratch_shapes=[
            pltpu.VMEM((N, slots, N, HD), bf),
            pltpu.VMEM((N, slots, N, HD), bf),
            pltpu.VMEM((N, 2, N // 2, ROWS, 2 * HD), bf),
            pltpu.VMEM((N, 16, GQ * HD), bf),
            pltpu.VMEM((N, 16, GQ * HD), bf),
            pltpu.VMEM((7, 4, ROWS, 2 * HD), bf),
            pltpu.VMEM((4, N, ROWS, 2 * HD), bf),
            pltpu.VMEM((7, N, ROWS, 2 * HD), bf),
            pltpu.VMEM((FINAL, N * ROWS, 2 * HD), bf),
            pltpu.VMEM((q_rows, HD), bf),
            pltpu.VMEM((q_rows, HD), bf),
            pltpu.VMEM((q_rows, HD), f32),
            pltpu.VMEM((q_rows, HD), f32),
            pltpu.VMEM((q_rows, HD), f32),
            pltpu.VMEM((q_rows, HD), f32),
            pltpu.VMEM((N, 16, GQ * HD), bf),
            pltpu.VMEM((N, 16, GQ * HD), bf),
            dma((7,)), dma((7,)), dma((7,)), dma((7,)),
            dma((7,)), dma((7,)), dma((4, N)), dma((4, N)),
            dma((3, N)), dma((3, N)), dma((4, 7)), dma((4, 7)),
            dma((PARTS, 7)), dma((PARTS, 7)), dma((PARTS, 7)), dma((PARTS, 7)),
            dma((N,)), dma((N,)), dma((2 + 2 * PARTS,)),
        ],
        compiler_params=pltpu.CompilerParams(
            collective_id=0, has_side_effects=True, vmem_limit_bytes=60 * 2 ** 20),
        cost_estimate=pl.CostEstimate(flops=8_000_000_000, bytes_accessed=8_000_000, transcendentals=7_000_000),
    )(image_tiles, text_len, queries, out_grad, q_gain.reshape(1, HD), k_gain.reshape(1, HD), keys, values)

    return tuple(pl.pallas_call(
        place,
        name="place_results",
        out_shape=(out, out),
        in_specs=[vmem, vmem],
        out_specs=(vmem, vmem),
        compiler_params=pltpu.CompilerParams(vmem_limit_bytes=60 * 2 ** 20),
    )(attention, query_grad))


def solution(mesh):
    return jax.shard_map(
        local,
        mesh=mesh,
        in_specs=(
            P("dp", "heads", None),
            P("dp", "heads", None),
            P(),
            P(),
            P(None, "dp", "heads"),
            P(None, "dp", "heads"),
            P(),
            P(),
        ),
        out_specs=(P("dp", "heads", None), P("dp", "heads", None)),
        check_vma=False,
    )
```
